512 devices in a mesh: mp: 16 (over x, y), dp: 32 (over z, core).
Axes of the slice: x: 4, y: 4, z: 16, core: 2. Of those that a mesh axis runs over, the one named last changes fastest.
Arguments:
- inputs: bfloat16 [5120, 8192], P('dp'), may hold values from -60 to 60
- cotangent: bfloat16 [5120, 16384], P('dp', 'mp'), may hold values from -11 to 11
- weight: float32 [8192, 16384], P('dp', 'mp'), may hold values from -6 to 6
- row_moment: float32 [8192], P('dp'), may hold values from 0.05 to 0.5
- col_moment: float32 [16384], P('mp'), may hold values from 0.01 to 60
Outputs:
- new_weight: float32 [8192, 16384], P('dp', 'mp')
- update: bfloat16 [8192, 16384], P('dp', 'mp')
- new_rows: float32 [8192], P('dp')
- new_cols: float32 [16384], P('mp')
The draws below stay inside these ranges and needn't reach their ends.
All inputs are finite; a program needn't handle non-finite values.
Results may differ from the reference program's by a relative error of at most 0.001.
Values may be sent and summed in bfloat16 or wider, within the bound.
No kernel may reach another device: no remote copies, remote signals or barrier semaphores. Data moves between devices by JAX's collectives and lax.ppermute only.
A program may use at most 64 MiB of HBM per device.

```python
import math
import jax
import jax.numpy as jnp
from jax import lax

D = 8192
F = 16384
TOKENS = 5120


def scaled_field(key, rows, cols, factor):
    first, second, third = jax.random.split(key, 3)
    noise = jnp.clip(jax.random.normal(first, (rows, cols), jnp.float32), -4.0, 4.0)
    row_scale = jnp.exp(jax.random.uniform(second, (rows, 1), jnp.float32) * jnp.log(10.0)) / jnp.sqrt(10.0)
    ramp = 0.5 + jnp.arange(cols, dtype=jnp.float32) / cols
    col_scale = jnp.exp(jax.random.uniform(third, (1, cols), jnp.float32) * jnp.log(10.0)) / jnp.sqrt(10.0) * ramp
    return noise * row_scale * col_scale * factor


def draw_inputs(key, part):
    key = jax.random.fold_in(key, 11)
    return scaled_field(key, TOKENS, D, 1.0).astype(jnp.bfloat16)


def draw_cotangent(key, part):
    key = jax.random.fold_in(key, 23)
    factor = 0.7 / jnp.sqrt(jnp.float32(TOKENS))
    return scaled_field(key, TOKENS, F, factor).astype(jnp.bfloat16)


def draw_col_moment(key, part):
    key = jax.random.fold_in(key, 37)
    position = jnp.arange(F, dtype=jnp.float32) / F
    jitter = jnp.exp(jax.random.uniform(key, (F,), jnp.float32, -1.0, 1.0) * jnp.log(2.0))
    level = 1.3 - 2.6 * position
    return (jnp.exp(level * jnp.log(10.0)) * jitter).astype(jnp.float32)


def level_of(own_key, dims, shards, smallest, high):
    factor_of, own = 1.0, jax.random.fold_in(own_key, 6)
    for dim, blocks in shards:
        steps = jnp.exp(jax.random.uniform(jax.random.fold_in(own, dim), (blocks,), jnp.float32, smallest / len(shards), high / len(shards)))
        factor_of = factor_of * jnp.repeat(steps, dims[dim] // blocks).reshape([-1 if axis == dim else 1 for axis in range(len(dims))])
    return factor_of


def bell_draw(rng, shape, spread, reach, cuts=(), kind=jnp.bfloat16):
    array = jax.random.normal(rng, shape, jnp.float32) * spread
    if len(cuts) > 0:
        array = level_of(rng, shape, cuts, -0.22, 0.18) * array
    return jnp.clip(array, min=-reach, max=reach).astype(kind)


def setup_inputs(seed: int = 0) -> dict:
    key_of = jax.random.split(jax.random.key(seed), 6)
    inputs = draw_inputs(jax.random.fold_in(key_of[5], 71), 0)
    cotangent = draw_cotangent(jax.random.fold_in(key_of[5], 71), 0)
    weight = bell_draw(key_of[2], (D, F), 1.0, 6.0, ((0, 32), (1, 16)), jnp.float32)
    row_moment = jnp.clip(jnp.exp(math.log(0.5) - 2.3025851 * jax.random.uniform(key_of[3], (D,), jnp.float32) ** level_of(key_of[3], (D,), ((0, 32),), -0.2, 0.2)), 0.05, 0.5)
    col_moment = draw_col_moment(jax.random.fold_in(key_of[5], 71), 0)
    return {"inputs": inputs, "cotangent": cotangent, "weight": weight, "row_moment": row_moment, "col_moment": col_moment}


decay_rate = 1.0 - 10.0 ** (-0.8)
step_size = 0.05
tiny_eps = 1e-30

def reference(inputs, cotangent, weight, row_moment, col_moment):
    gradient = jnp.dot(inputs.T, cotangent, preferred_element_type=jnp.float32)
    squares = gradient * gradient + tiny_eps
    new_rows = decay_rate * row_moment + (1.0 - decay_rate) * (lax.optimization_barrier(jnp.sum(squares, axis=1)) / F)
    new_cols = decay_rate * col_moment + (1.0 - decay_rate) * (lax.optimization_barrier(jnp.sum(squares, axis=0)) / D)
    row_mean = jnp.sum(new_rows) / D
    scaled = gradient / jnp.sqrt(new_rows[:, None] * new_cols[None, :] / row_mean)
    update_rms = jnp.sqrt(jnp.sum(scaled * scaled) / (D * F))
    clipped = scaled / jnp.maximum(1.0, update_rms)
    weight_rms = jnp.sqrt(jnp.sum(weight * weight) / (D * F))
    new_weight = weight - step_size * weight_rms * clipped
    return (new_weight, clipped.astype(jnp.bfloat16), new_rows, new_cols)
```

```python
import jax
import jax.numpy as jnp
from jax import lax
from jax.sharding import Mesh, PartitionSpec as P

D = 8192
F = 16384

decay_rate = 1.0 - 10.0 ** (-0.8)
step_size = 0.05
tiny_eps = 1e-30

NX, NY, NZ = 4, 4, 16
XY, ZC = ("x", "y"), ("z", "c")


def contract(left, right):
    return lax.dot_general(
        left, right, (((0,), (0,)), ((), ())), preferred_element_type=jnp.float32
    )


def shift(n, k):
    return [(i, (i + k) % n) for i in range(n)]


def gather_ring(block, axis, n):
    me = lax.axis_index(axis)
    out = jnp.zeros((n,) + block.shape, block.dtype)
    out = lax.dynamic_update_index_in_dim(out, block, me, 0)
    for k in range(1, n):
        got = lax.ppermute(block, axis, shift(n, k))
        out = lax.dynamic_update_index_in_dim(out, got, lax.rem(me + n - k, n), 0)
    return out


def sum_over(value, axes, n):
    copies = jnp.broadcast_to(value[None], (n,) + value.shape)
    return jnp.sum(lax.all_to_all(copies, axes, 0, 0), axis=0)


def features_of_rows(inputs):
    x, y, c = lax.axis_index("x"), lax.axis_index("y"), lax.axis_index("c")
    tokens = inputs.shape[0] // NY
    part = lax.dynamic_slice_in_dim(inputs, y * tokens, tokens, 0)
    part = part.reshape(tokens, NZ, NX, 128)
    part = lax.dynamic_index_in_dim(part, x, 2, keepdims=False)
    part = lax.all_to_all(part.transpose(1, 0, 2), "z", 0, 0)
    part = gather_ring(part, "x", NX)
    part = gather_ring(part, "y", NY)
    own = lax.dynamic_slice_in_dim(part, 2 * c, 2, 1)
    other = lax.dynamic_slice_in_dim(part, 2 - 2 * c, 2, 1)
    other = lax.ppermute(other, "c", shift(2, 1))
    both = jnp.where(c == 0, jnp.stack([own, other]), jnp.stack([other, own]))
    both = both.transpose(3, 0, 1, 4, 2, 5)
    return both.reshape(NZ * 2 * NY * tokens, 256)


def on_device(inputs, cotangent, weight, row_moment, col_moment):
    all_cotangent = lax.all_gather(cotangent, ZC, axis=0, tiled=True)
    feat_rows = features_of_rows(inputs)
    weight_sq = jnp.sum(weight * weight)
    gradient = contract(feat_rows, all_cotangent)
    squares = gradient * gradient + tiny_eps
    row_total = sum_over(jnp.sum(squares, axis=1), XY, NX * NY)
    new_rows = decay_rate * row_moment + (1.0 - decay_rate) * (row_total / F)
    weighted = jnp.sum(gradient * gradient / new_rows[:, None], axis=0)
    scalars = jnp.stack([jnp.sum(new_rows), weight_sq])
    packed = jnp.concatenate([jnp.sum(squares, axis=0), weighted, jnp.pad(scalars, (0, 126))])
    packed = sum_over(lax.psum(packed.reshape(-1, 128), "c"), "z", NZ).reshape(-1)
    col_total, weighted = packed[:1024], packed[1024:2048]
    row_mean = packed[2048] / D
    new_cols = decay_rate * col_moment + (1.0 - decay_rate) * (col_total / D)
    lanes = jnp.arange(128)
    last = jnp.where(lanes == 0, jnp.sum(weighted / new_cols), jnp.where(lanes == 1, packed[2049], 0.0))
    last = sum_over(last[None], XY, NX * NY)[0]
    update_rms = jnp.sqrt(row_mean * last[0] / (D * F))
    weight_rms = jnp.sqrt(last[1] / (D * F))
    row_factor = jnp.sqrt(row_mean) / jnp.maximum(1.0, update_rms) / jnp.sqrt(new_rows)
    clipped = gradient * row_factor[:, None] * (1.0 / jnp.sqrt(new_cols))[None, :]
    new_weight = weight - step_size * weight_rms * clipped
    return (new_weight, clipped.astype(jnp.bfloat16), new_rows, new_cols)


def solution(mesh):
    fine = Mesh(mesh.devices.reshape(NX, NY, NZ, 2), ("x", "y", "z", "c"))
    return jax.shard_map(
        on_device,
        mesh=fine,
        in_specs=(P(ZC, None), P(ZC, XY), P(ZC, XY), P(ZC), P(XY)),
        out_specs=(P(ZC, XY), P(ZC, XY), P(ZC), P(XY)),
        check_vma=False,
    )
```

```python
import jax
import jax.numpy as jnp
from jax import lax
from jax.sharding import Mesh, PartitionSpec as P

D = 8192
F = 16384

decay_rate = 1.0 - 10.0 ** (-0.8)
step_size = 0.05
tiny_eps = 1e-30

NX, NY, NZ = 4, 4, 16
XY, ZC = ("x", "y"), ("z", "c")


def contract(left, right):
    return lax.dot_general(
        left, right, (((0,), (0,)), ((), ())), preferred_element_type=jnp.float32
    )


def shift(n, k):
    return [(i, (i + k) % n) for i in range(n)]


def sum_over(value, axes, n):
    copies = jnp.broadcast_to(value[None], (n,) + value.shape)
    return jnp.sum(lax.all_to_all(copies, axes, 0, 0), axis=0)


def features_of_rows(inputs):
    x, y, c = lax.axis_index("x"), lax.axis_index("y"), lax.axis_index("c")
    tokens = inputs.shape[0] // NY
    part = lax.dynamic_slice_in_dim(inputs, y * tokens, tokens, 0)
    part = part.reshape(tokens, NZ, NX, 128)
    part = lax.dynamic_index_in_dim(part, x, 2, keepdims=False)
    part = lax.all_to_all(part.transpose(1, 0, 2), "z", 0, 0)
    part = lax.all_gather(part, "x", axis=0)
    low, high = part[:2], part[2:]
    own = jnp.where(c == 0, low, high)
    other = lax.ppermute(jnp.where(c == 0, high, low), "c", shift(2, 1))
    first, second = jnp.where(c == 0, own, other), jnp.where(c == 0, other, own)
    both = jnp.stack([first, second]).transpose(2, 0, 3, 1, 4)
    both = both.reshape(NZ, 2, tokens, 256)
    groups = [both] + [lax.ppermute(both, "y", shift(NY, k)) for k in range(1, NY)]
    return jnp.concatenate(groups, axis=2).reshape(NZ * 2 * NY * tokens, 256)


def rotated(cotangent):
    y = lax.axis_index("y")
    groups = cotangent.reshape(NY, -1, cotangent.shape[1])
    backward = jnp.concatenate([groups[::-1], groups[::-1][:3]])
    return lax.dynamic_slice_in_dim(backward, 3 - y, NY, 0).reshape(cotangent.shape)


def on_device(inputs, cotangent, weight, row_moment, col_moment):
    c = lax.axis_index("c")
    all_cotangent = lax.all_gather(rotated(cotangent), ZC, axis=0, tiled=True)
    feat_rows = features_of_rows(inputs)
    weight_sq = jnp.sum(weight * weight)
    gradient = contract(feat_rows, all_cotangent)
    squares = gradient * gradient + tiny_eps
    row_total = sum_over(jnp.sum(squares, axis=1)[None], XY, NX * NY)[0]
    new_rows = decay_rate * row_moment + (1.0 - decay_rate) * (row_total / F)
    weighted = jnp.sum(gradient * gradient / new_rows[:, None], axis=0)
    scalars = jnp.pad(jnp.stack([jnp.sum(new_rows), weight_sq]), (0, 126))
    columns = jnp.stack([jnp.sum(squares, axis=0), weighted])
    columns = columns.reshape(2, 2, 512).transpose(1, 0, 2).reshape(2, 1024)
    packed = jnp.concatenate([columns, jnp.stack([scalars, scalars])], axis=1)
    packed = lax.dynamic_slice_in_dim(lax.psum(packed, "c"), c, 1, 0)
    packed = sum_over(packed, "z", NZ)[0]
    row_mean = packed[1024] / D
    half_moment = lax.dynamic_slice_in_dim(col_moment, c * 512, 512, 0)
    half_cols = decay_rate * half_moment + (1.0 - decay_rate) * (packed[:512] / D)
    new_cols = lax.all_gather(half_cols, "c", axis=0, tiled=True)
    lanes = jnp.arange(128)
    scaled_sq = row_mean * jnp.sum(packed[512:1024] / half_cols)
    last = jnp.where(lanes == 0, scaled_sq, jnp.where(lanes == 1, 0.5 * packed[1025], 0.0))
    last = sum_over(last[None], ("x", "y", "c"), NX * NY * 2)[0]
    update_rms = jnp.sqrt(last[0] / (D * F))
    weight_rms = jnp.sqrt(last[1] / (D * F))
    row_factor = jnp.sqrt(row_mean) / jnp.maximum(1.0, update_rms) / jnp.sqrt(new_rows)
    clipped = gradient * row_factor[:, None] * (1.0 / jnp.sqrt(new_cols))[None, :]
    new_weight = weight - step_size * weight_rms * clipped
    return (new_weight, clipped.astype(jnp.bfloat16), new_rows, new_cols)


def solution(mesh):
    fine = Mesh(mesh.devices.reshape(NX, NY, NZ, 2), ("x", "y", "z", "c"))
    return jax.shard_map(
        on_device,
        mesh=fine,
        in_specs=(P(ZC, None), P(ZC, XY), P(ZC, XY), P(ZC), P(XY)),
        out_specs=(P(ZC, XY), P(ZC, XY), P(ZC), P(XY)),
        check_vma=False,
    )
```

```python
import jax
import jax.numpy as jnp
from jax import lax
from jax.experimental import pallas as pl
from jax.experimental.pallas import tpu as pltpu
from jax.sharding import Mesh, PartitionSpec as P

D = 8192
F = 16384

decay_rate = 1.0 - 10.0 ** (-0.8)
step_size = 0.05
tiny_eps = 1e-30

NX, NY, NZ = 4, 4, 16
XY, ZC = ("x", "y"), ("z", "c")


def pairs(n, flip):
    return [(i, i ^ flip) for i in range(n)]


def in_order(y, own, one, two, three):
    odd, upper = (y & 1) == 1, (y & 2) == 2
    near = [jnp.where(odd, one, own), jnp.where(odd, own, one)]
    far = [jnp.where(odd, three, two), jnp.where(odd, two, three)]
    first = [jnp.where(upper, q, p) for p, q in zip(near, far)]
    second = [jnp.where(upper, p, q) for p, q in zip(near, far)]
    return jnp.concatenate(first + second, axis=2)


def features_of_rows(inputs, weight_sq):
    x, y, c = lax.axis_index("x"), lax.axis_index("y"), lax.axis_index("c")
    tokens = inputs.shape[0] // NY
    part = lax.dynamic_slice_in_dim(inputs, y * tokens, tokens, 0)
    part = part.reshape(tokens, NZ, NX, 128)
    part = lax.dynamic_index_in_dim(part, x, 2, keepdims=False)
    part = lax.all_to_all(part.transpose(1, 0, 2), "z", 0, 0)
    part, weight_sq = lax.optimization_barrier((part, weight_sq))
    part = lax.all_gather(part, "x", axis=0)
    low, high = part[:2], part[2:]
    own = jnp.where(c == 0, low, high)
    other = lax.ppermute(jnp.where(c == 0, high, low), "c", pairs(2, 1))
    first, second = jnp.where(c == 0, own, other), jnp.where(c == 0, other, own)

    def swap(block, flip):
        return lax.ppermute(block, "y", pairs(NY, flip))

    first_one, second_three = swap(first, 1), swap(second, 3)
    first_three, second_one = swap(first, 3), swap(second, 1)
    first_two, second_two = swap(first_one, 3), swap(second_three, 1)
    return (
        in_order(y, first, first_one, first_two, first_three),
        in_order(y, second, second_one, second_two, second_three),
        weight_sq,
    )


PLANES = 4


def gradient_kernel(first_ref, second_ref, cot_ref, grad_ref, rows_ref):
    step = pl.program_id(0)

    @pl.when(step == 0)
    def _():
        grad_ref[...] = jnp.zeros_like(grad_ref)

    feat = [
        jnp.concatenate([ref[0, plane], ref[1, plane]], axis=1)
        for plane in range(PLANES)
        for ref in (first_ref, second_ref)
    ]
    grad_ref[...] += lax.dot_general(
        jnp.concatenate(feat, axis=0),
        cot_ref[...].reshape(PLANES * 320, 1024),
        (((0,), (0,)), ((), ())),
        preferred_element_type=jnp.float32,
    )

    @pl.when(step == pl.num_programs(0) - 1)
    def _():
        squares = jnp.zeros((256, 128), jnp.float32)
        for j in range(8):
            part = grad_ref[:, j * 128 : (j + 1) * 128]
            squares += part * part + tiny_eps
        row = jnp.sum(squares.T, axis=0, keepdims=True)
        for i in range(NX * NY):
            rows_ref[i] = row


LARGE = pltpu.CompilerParams(vmem_limit_bytes=56 * 2**20)
SMALL = pltpu.CompilerParams(vmem_limit_bytes=16 * 2**20)


def gradient_of(first, second, all_cotangent):
    feat_spec = pl.BlockSpec((2, PLANES, 160, 128), lambda i: (0, i, 0, 0))
    return pl.pallas_call(
        gradient_kernel,
        grid=(NZ // PLANES,),
        in_specs=[feat_spec, feat_spec, pl.BlockSpec((PLANES, 2, 160, 1024), lambda i: (i, 0, 0, 0))],
        out_specs=[
            pl.BlockSpec((256, 1024), lambda i: (0, 0)),
            pl.BlockSpec((NX * NY, 1, 256), lambda i: (0, 0, 0)),
        ],
        out_shape=[
            jax.ShapeDtypeStruct((256, 1024), jnp.float32),
            jax.ShapeDtypeStruct((NX * NY, 1, 256), jnp.float32),
        ],
        cost_estimate=pl.CostEstimate(
            flops=2 * 256 * 1024 * 5120, bytes_accessed=15_000_000, transcendentals=0
        ),
        compiler_params=LARGE,
        name="gradient",
    )(first, second, all_cotangent)


def rows_kernel(
    got_ref, moment_ref, weight_sq_ref, grad_hbm, new_rows_ref, factor_ref, out_ref, grad, sem
):
    fetch = pltpu.make_async_copy(grad_hbm, grad, sem)
    fetch.start()
    total = jnp.sum(got_ref[...], axis=0)
    new_rows = decay_rate * moment_ref[...] + (1.0 - decay_rate) * (total / F)
    new_rows_ref[...] = new_rows
    down = jnp.broadcast_to(new_rows, (128, 256)).T
    factor_ref[...] = lax.rsqrt(down)
    inverse = 1.0 / down
    lanes = lax.broadcasted_iota(jnp.int32, (1, 128), 1)
    rows_sum = jnp.sum(new_rows, axis=1, keepdims=True)
    scalars = jnp.where(lanes == 0, rows_sum, jnp.where(lanes == 1, weight_sq_ref[0, 0], 0.0))
    fetch.wait()
    squares, weighted = [], []
    for j in range(8):
        part = grad[:, j * 128 : (j + 1) * 128]
        part = part * part
        squares.append(jnp.sum(part + tiny_eps, axis=0, keepdims=True))
        weighted.append(jnp.sum(part * inverse, axis=0, keepdims=True))
    for half in range(2):
        mine = slice(4 * half, 4 * half + 4)
        out_ref[half : half + 1] = jnp.concatenate(squares[mine] + weighted[mine] + [scalars], axis=1)


VMEM = pl.BlockSpec(memory_space=pltpu.VMEM)
SMEM = pl.BlockSpec(memory_space=pltpu.SMEM)
HBM = pl.BlockSpec(memory_space=pltpu.HBM)


def rows_call(row_sums, row_moment, weight_sq, gradient):
    return pl.pallas_call(
        rows_kernel,
        in_specs=[VMEM, VMEM, SMEM, HBM],
        out_specs=[VMEM] * 3,
        out_shape=[
            jax.ShapeDtypeStruct((1, 256), jnp.float32),
            jax.ShapeDtypeStruct((256, 128), jnp.float32),
            jax.ShapeDtypeStruct((2, 1152), jnp.float32),
        ],
        scratch_shapes=[pltpu.VMEM((256, 1024), jnp.float32), pltpu.SemaphoreType.DMA],
        compiler_params=SMALL,
        name="rows",
    )(row_sums, row_moment, weight_sq, gradient)


def columns_kernel(got_ref, moment_ref, new_cols_ref, scalars_ref, out_ref):
    total = jnp.sum(got_ref[...], axis=0)
    new_cols = decay_rate * moment_ref[...] + (1.0 - decay_rate) * (total[:, :512] / D)
    new_cols_ref[...] = new_cols
    row_mean = total[:, 1024:1025] / D
    scaled_sq = row_mean * jnp.sum(total[:, 512:1024] / new_cols, axis=1, keepdims=True)
    lanes = lax.broadcasted_iota(jnp.int32, (1, 128), 1)
    scalars_ref[...] = jnp.broadcast_to(row_mean, (1, 128))
    half_sq = 0.5 * total[:, 1025:1026]
    row = jnp.where(lanes == 0, scaled_sq, jnp.where(lanes == 1, half_sq, 0.0))
    for i in range(2 * NX * NY):
        out_ref[i] = row


def columns_call(packed, half_moment):
    return pl.pallas_call(
        columns_kernel,
        in_specs=[VMEM] * 2,
        out_specs=[VMEM] * 3,
        out_shape=[
            jax.ShapeDtypeStruct((1, 512), jnp.float32),
            jax.ShapeDtypeStruct((1, 128), jnp.float32),
            jax.ShapeDtypeStruct((2 * NX * NY, 1, 128), jnp.float32),
        ],
        compiler_params=SMALL,
        name="columns",
    )(packed, half_moment)


PARTS = 4


def update_kernel(
    got_ref, mean_ref, factor_ref, cols_ref, grad_hbm, weight_hbm, new_weight_hbm, update_hbm,
    cols_hbm, grad, weight, new_weight, update, in_sems, out_sems, cols_sem,
):
    height = 256 // PARTS
    blocks = [pl.ds(i * height, height) for i in range(PARTS)]
    fetches, stores = [], []
    for i, rows in enumerate(blocks):
        fetches.append(pltpu.make_async_copy(grad_hbm.at[rows], grad.at[rows], in_sems.at[0, i]))
        fetches.append(pltpu.make_async_copy(weight_hbm.at[rows], weight.at[rows], in_sems.at[1, i]))
    for fetch in fetches:
        fetch.start()
    stores.append(pltpu.make_async_copy(cols_ref, cols_hbm, cols_sem))
    stores[0].start()
    total = jnp.sum(got_ref[...], axis=0)
    update_rms = jnp.sqrt(total[:, 0:1] / (D * F))
    weight_rms = jnp.sqrt(total[:, 1:2] / (D * F))
    scale = jnp.sqrt(mean_ref[:, 0:1]) / jnp.maximum(1.0, update_rms)
    step = step_size * weight_rms
    cols = [lax.rsqrt(cols_ref[half]) * scale for half in range(2)]
    for i, rows in enumerate(blocks):
        fetches[2 * i].wait()
        fetches[2 * i + 1].wait()
        factor = factor_ref[rows]
        for j in range(8):
            here = slice(j * 128, (j + 1) * 128)
            half = slice((j % 4) * 128, (j % 4 + 1) * 128)
            clipped = grad[rows, here] * factor * cols[j // 4][:, half]
            update[rows, here] = clipped.astype(jnp.bfloat16)
            new_weight[rows, here] = weight[rows, here] - step * clipped
        out = [
            pltpu.make_async_copy(new_weight.at[rows], new_weight_hbm.at[rows], out_sems.at[0, i]),
            pltpu.make_async_copy(update.at[rows], update_hbm.at[rows], out_sems.at[1, i]),
        ]
        for store in out:
            store.start()
        stores += out
    for store in stores:
        store.wait()


def update_call(last, row_mean, row_factor, new_cols, gradient, weight):
    whole = lambda dtype: pltpu.VMEM((256, 1024), dtype)
    return pl.pallas_call(
        update_kernel,
        in_specs=[VMEM] * 4 + [HBM] * 2,
        out_specs=[HBM] * 3,
        out_shape=[
            jax.ShapeDtypeStruct((256, 1024), jnp.float32),
            jax.ShapeDtypeStruct((256, 1024), jnp.bfloat16),
            jax.ShapeDtypeStruct((2, 1, 512), jnp.float32),
        ],
        scratch_shapes=[
            whole(jnp.float32),
            whole(jnp.float32),
            whole(jnp.float32),
            whole(jnp.bfloat16),
            pltpu.SemaphoreType.DMA((2, PARTS)),
            pltpu.SemaphoreType.DMA((2, PARTS)),
            pltpu.SemaphoreType.DMA,
        ],
        compiler_params=SMALL,
        name="update",
    )(last, row_mean, row_factor, new_cols, gradient, weight)


def on_device(inputs, cotangent, weight, row_moment, col_moment):
    c = lax.axis_index("c")
    all_cotangent = lax.all_gather(cotangent, ZC, axis=0).reshape(NZ, 2, *cotangent.shape)
    first, second, weight_sq = features_of_rows(inputs, jnp.sum(weight * weight))
    gradient, row_sums = gradient_of(first, second, all_cotangent)
    row_sums = lax.all_to_all(row_sums, XY, 0, 0)
    new_rows, row_factor, packed = rows_call(
        row_sums, row_moment[None], weight_sq.reshape(1, 1), gradient
    )
    packed = lax.dynamic_slice_in_dim(lax.psum(packed, "c"), c, 1, 0)
    packed = lax.all_to_all(jnp.broadcast_to(packed[None], (NZ, 1, 1152)), "z", 0, 0)
    half_moment = jnp.where(c == 0, col_moment[:512], col_moment[512:])
    half_cols, row_mean, last = columns_call(packed, half_moment[None])
    last = lax.all_to_all(last, ("x", "y", "c"), 0, 0)
    new_cols = lax.all_gather(half_cols, "c", axis=0)
    new_weight, update, new_cols = update_call(last, row_mean, row_factor, new_cols, gradient, weight)
    return (new_weight, update, new_rows[0], new_cols.reshape(1024))


def solution(mesh):
    fine = Mesh(mesh.devices.reshape(NX, NY, NZ, 2), ("x", "y", "z", "c"))
    return jax.shard_map(
        on_device,
        mesh=fine,
        in_specs=(P(ZC, None), P(ZC, XY), P(ZC, XY), P(ZC), P(XY)),
        out_specs=(P(ZC, XY), P(ZC, XY), P(ZC), P(XY)),
        check_vma=False,
    )
```

```python
import jax
import jax.numpy as jnp
from jax import lax
from jax.experimental import pallas as pl
from jax.experimental.pallas import tpu as pltpu
from jax.sharding import Mesh, PartitionSpec as P

D = 8192
F = 16384

decay_rate = 1.0 - 10.0 ** (-0.8)
step_size = 0.05
tiny_eps = 1e-30

NX, NY, NZ = 4, 4, 16
XY, ZC = ("x", "y"), ("z", "c")


def pairs(n, flip):
    return [(i, i ^ flip) for i in range(n)]


def in_order(y, own, one, two, three):
    odd, upper = (y & 1) == 1, (y & 2) == 2
    near = [jnp.where(odd, one, own), jnp.where(odd, own, one)]
    far = [jnp.where(odd, three, two), jnp.where(odd, two, three)]
    first = [jnp.where(upper, q, p) for p, q in zip(near, far)]
    second = [jnp.where(upper, p, q) for p, q in zip(near, far)]
    return jnp.concatenate(first + second, axis=2)


def features_of_rows(inputs, early):
    x, y, c = lax.axis_index("x"), lax.axis_index("y"), lax.axis_index("c")
    tokens = inputs.shape[0] // NY
    part = lax.dynamic_slice_in_dim(inputs, y * tokens, tokens, 0)
    part = part.reshape(tokens, NZ, NX, 128)
    part = lax.dynamic_index_in_dim(part, x, 2, keepdims=False)
    part = lax.all_to_all(part.transpose(1, 0, 2), "z", 0, 0)
    part, early = lax.optimization_barrier((part, early))
    part = lax.all_gather(part, "x", axis=0)
    low, high = part[:2], part[2:]
    own = jnp.where(c == 0, low, high)
    other = lax.ppermute(jnp.where(c == 0, high, low), "c", pairs(2, 1))
    first, second = jnp.where(c == 0, own, other), jnp.where(c == 0, other, own)

    def swap(block, flip):
        return lax.ppermute(block, "y", pairs(NY, flip))

    first_one, second_three = swap(first, 1), swap(second, 3)
    first_three, second_one = swap(first, 3), swap(second, 1)
    first_two, second_two = swap(first_one, 3), swap(second_three, 1)
    return (
        in_order(y, first, first_one, first_two, first_three),
        in_order(y, second, second_one, second_two, second_three),
        early,
    )


PLANES = 4


def gradient_kernel(core_ref, first_ref, second_ref, cot_ref, grad_ref, rows_ref, other_ref):
    step = pl.program_id(0)

    @pl.when(step == 0)
    def _():
        grad_ref[...] = jnp.zeros_like(grad_ref)

    feat = [
        jnp.concatenate([ref[0, plane], ref[1, plane]], axis=1)
        for plane in range(PLANES)
        for ref in (first_ref, second_ref)
    ]
    grad_ref[...] += lax.dot_general(
        jnp.concatenate(feat, axis=0),
        cot_ref[...].reshape(PLANES * 320, 1024),
        (((0,), (0,)), ((), ())),
        preferred_element_type=jnp.float32,
    )

    @pl.when(step == pl.num_programs(0) - 1)
    def _():
        squares = jnp.zeros((256, 128), jnp.float32)
        for j in range(8):
            part = grad_ref[:, j * 128 : (j + 1) * 128]
            squares += part * part + tiny_eps
        row = jnp.sum(squares.T, axis=0, keepdims=True)
        for i in range(2 * NX * NY):
            rows_ref[i] = row
        other_ref[...] = grad_ref[:, pl.ds(pl.multiple_of(512 * (1 - core_ref[0, 0]), 512), 512)]


LARGE = pltpu.CompilerParams(vmem_limit_bytes=56 * 2**20)
STREAM = pltpu.CompilerParams(vmem_limit_bytes=52 * 2**20 + 943_104)
SMALL = pltpu.CompilerParams(vmem_limit_bytes=16 * 2**20)


VMEM = pl.BlockSpec(memory_space=pltpu.VMEM)
SMEM = pl.BlockSpec(memory_space=pltpu.SMEM)
HBM = pl.BlockSpec(memory_space=pltpu.HBM)


def gradient_of(core, first, second, all_cotangent):
    feat_spec = pl.BlockSpec((2, PLANES, 160, 128), lambda i: (0, i, 0, 0))
    cot_spec = pl.BlockSpec((PLANES, 2, 160, 1024), lambda i: (i, 0, 0, 0))
    return pl.pallas_call(
        gradient_kernel,
        grid=(NZ // PLANES,),
        in_specs=[SMEM, feat_spec, feat_spec, cot_spec],
        out_specs=[
            pl.BlockSpec((256, 1024), lambda i: (0, 0)),
            pl.BlockSpec((2 * NX * NY, 1, 256), lambda i: (0, 0, 0)),
            pl.BlockSpec((256, 512), lambda i: (0, 0)),
        ],
        out_shape=[
            jax.ShapeDtypeStruct((256, 1024), jnp.float32),
            jax.ShapeDtypeStruct((2 * NX * NY, 1, 256), jnp.float32),
            jax.ShapeDtypeStruct((256, 512), jnp.float32),
        ],
        cost_estimate=pl.CostEstimate(
            flops=2 * 256 * 1024 * 5120, bytes_accessed=15_000_000, transcendentals=0
        ),
        compiler_params=LARGE,
        name="gradient",
    )(core, first, second, all_cotangent)


def rows_kernel(
    core_ref, got_ref, moment_ref, weight_sq_ref, grad_hbm, swapped_ref, new_rows_ref, factor_ref, out_ref, grad, sem
):
    core = core_ref[0, 0]
    columns = pl.ds(pl.multiple_of(512 * core, 512), 512)
    fetch = pltpu.make_async_copy(grad_hbm.at[:, columns], grad, sem)
    fetch.start()
    new_rows = []
    for half in range(2):
        total = got_ref[half]
        for i in range(1, NX * NY):
            total += got_ref[2 * i + half]
        new_rows.append(decay_rate * moment_ref[half] + (1.0 - decay_rate) * (total / F))
    own = jnp.where(core == 0, new_rows[0], new_rows[1])
    other = jnp.where(core == 0, new_rows[1], new_rows[0])
    new_rows_ref[...] = own
    down = jnp.broadcast_to(own, (128, 256)).T
    factor_ref[...] = lax.rsqrt(down)
    inverse = 1.0 / down
    inverse_other = 1.0 / jnp.broadcast_to(other, (128, 256)).T
    lanes = lax.broadcasted_iota(jnp.int32, (1, 128), 1)
    rows_sum = jnp.sum(own + other, axis=1, keepdims=True)
    scalars = jnp.where(lanes == 0, rows_sum, jnp.where(lanes == 1, weight_sq_ref[0, 0], 0.0))
    fetch.wait()
    squares, weighted = [], []
    for j in range(4):
        here = slice(128 * j, 128 * (j + 1))
        mine, theirs = grad[:, here], swapped_ref[:, here]
        mine, theirs = mine * mine, theirs * theirs
        squares.append(jnp.sum((mine + tiny_eps) + (theirs + tiny_eps), axis=0, keepdims=True))
        weighted.append(jnp.sum(mine * inverse + theirs * inverse_other, axis=0, keepdims=True))
    row = jnp.concatenate(squares + weighted + [scalars], axis=1)
    for i in range(NZ):
        out_ref[i] = row


def rows_call(core, row_sums, row_moment, weight_sq, gradient, swapped):
    return pl.pallas_call(
        rows_kernel,
        in_specs=[SMEM, VMEM, VMEM, SMEM, HBM, VMEM],
        out_specs=[VMEM] * 3,
        out_shape=[
            jax.ShapeDtypeStruct((1, 256), jnp.float32),
            jax.ShapeDtypeStruct((256, 128), jnp.float32),
            jax.ShapeDtypeStruct((NZ, 1, 1152), jnp.float32),
        ],
        scratch_shapes=[pltpu.VMEM((256, 512), jnp.float32), pltpu.SemaphoreType.DMA],
        compiler_params=STREAM,
        name="rows",
    )(core, row_sums, row_moment, weight_sq, gradient, swapped)


def columns_kernel(got_ref, moment_ref, new_cols_ref, scalars_ref, out_ref):
    total = jnp.sum(got_ref[...], axis=0)
    new_cols = decay_rate * moment_ref[...] + (1.0 - decay_rate) * (total[:, :512] / D)
    new_cols_ref[...] = new_cols
    row_mean = total[:, 1024:1025] / D
    scaled_sq = row_mean * jnp.sum(total[:, 512:1024] / new_cols, axis=1, keepdims=True)
    lanes = lax.broadcasted_iota(jnp.int32, (1, 128), 1)
    scalars_ref[...] = jnp.broadcast_to(row_mean, (1, 128))
    weight_sq = total[:, 1025:1026]
    row = jnp.where(lanes == 0, scaled_sq, jnp.where(lanes == 1, weight_sq, 0.0))
    for i in range(2 * NX * NY):
        out_ref[i] = row


def columns_call(packed, half_moment):
    return pl.pallas_call(
        columns_kernel,
        in_specs=[VMEM] * 2,
        out_specs=[VMEM] * 3,
        out_shape=[
            jax.ShapeDtypeStruct((1, 512), jnp.float32),
            jax.ShapeDtypeStruct((1, 128), jnp.float32),
            jax.ShapeDtypeStruct((2 * NX * NY, 1, 128), jnp.float32),
        ],
        compiler_params=SMALL,
        name="columns",
    )(packed, half_moment)


PARTS = 4


def update_kernel(
    got_ref, mean_ref, factor_ref, cols_ref, grad_hbm, weight_hbm, new_weight_hbm, update_hbm,
    cols_hbm, grad, weight, new_weight, update, in_sems, out_sems, cols_sem,
):
    height = 256 // PARTS
    blocks = [pl.ds(i * height, height) for i in range(PARTS)]
    fetches, stores = [], []
    for i, rows in enumerate(blocks):
        fetches.append(pltpu.make_async_copy(grad_hbm.at[rows], grad.at[rows], in_sems.at[0, i]))
        fetches.append(pltpu.make_async_copy(weight_hbm.at[rows], weight.at[rows], in_sems.at[1, i]))
    for fetch in fetches:
        fetch.start()
    stores.append(pltpu.make_async_copy(cols_ref, cols_hbm, cols_sem))
    stores[0].start()
    total = jnp.sum(got_ref[...], axis=0)
    update_rms = jnp.sqrt(total[:, 0:1] / (D * F))
    weight_rms = jnp.sqrt(total[:, 1:2] / (D * F))
    scale = jnp.sqrt(mean_ref[:, 0:1]) / jnp.maximum(1.0, update_rms)
    step = step_size * weight_rms
    cols = [lax.rsqrt(cols_ref[half]) * scale for half in range(2)]
    for i, rows in enumerate(blocks):
        fetches[2 * i].wait()
        fetches[2 * i + 1].wait()
        factor = factor_ref[rows]
        for j in range(8):
            here = slice(j * 128, (j + 1) * 128)
            half = slice((j % 4) * 128, (j % 4 + 1) * 128)
            clipped = grad[rows, here] * factor * cols[j // 4][:, half]
            update[rows, here] = clipped.astype(jnp.bfloat16)
            new_weight[rows, here] = weight[rows, here] - step * clipped
        out = [
            pltpu.make_async_copy(new_weight.at[rows], new_weight_hbm.at[rows], out_sems.at[0, i]),
            pltpu.make_async_copy(update.at[rows], update_hbm.at[rows], out_sems.at[1, i]),
        ]
        for store in out:
            store.start()
        stores += out
    for store in stores:
        store.wait()


def update_call(last, row_mean, row_factor, new_cols, gradient, weight):
    whole = lambda dtype: pltpu.VMEM((256, 1024), dtype)
    return pl.pallas_call(
        update_kernel,
        in_specs=[VMEM] * 4 + [HBM] * 2,
        out_specs=[HBM] * 3,
        out_shape=[
            jax.ShapeDtypeStruct((256, 1024), jnp.float32),
            jax.ShapeDtypeStruct((256, 1024), jnp.bfloat16),
            jax.ShapeDtypeStruct((2, 1, 512), jnp.float32),
        ],
        scratch_shapes=[
            whole(jnp.float32),
            whole(jnp.float32),
            whole(jnp.float32),
            whole(jnp.bfloat16),
            pltpu.SemaphoreType.DMA((2, PARTS)),
            pltpu.SemaphoreType.DMA((2, PARTS)),
            pltpu.SemaphoreType.DMA,
        ],
        compiler_params=STREAM,
        name="update",
    )(last, row_mean, row_factor, new_cols, gradient, weight)


def on_device(inputs, cotangent, weight, row_moment, col_moment):
    c = lax.axis_index("c")
    core = c.astype(jnp.int32).reshape(1, 1)
    all_cotangent = lax.all_gather(cotangent, ZC, axis=0).reshape(NZ, 2, *cotangent.shape)
    early = (jnp.sum(weight * weight), lax.all_gather(row_moment[None], "c", axis=0))
    first, second, (weight_sq, row_moments) = features_of_rows(inputs, early)
    gradient, row_sums, swapped = gradient_of(core, first, second, all_cotangent)
    row_sums = lax.all_to_all(row_sums, ("x", "y", "c"), 0, 0)
    swapped = lax.ppermute(swapped, "c", pairs(2, 1))
    new_rows, row_factor, packed = rows_call(
        core, row_sums, row_moments, weight_sq.reshape(1, 1), gradient, swapped
    )
    packed = lax.all_to_all(packed, "z", 0, 0)
    half_moment = jnp.where(c == 0, col_moment[:512], col_moment[512:])
    half_cols, row_mean, last = columns_call(packed, half_moment[None])
    last = lax.all_to_all(last, ("x", "y", "c"), 0, 0)
    new_cols = lax.all_gather(half_cols, "c", axis=0)
    new_weight, update, new_cols = update_call(
        last, row_mean, row_factor, new_cols, gradient, weight
    )
    return (new_weight, update, new_rows[0], new_cols.reshape(1024))


def solution(mesh):
    fine = Mesh(mesh.devices.reshape(NX, NY, NZ, 2), ("x", "y", "z", "c"))
    return jax.shard_map(
        on_device,
        mesh=fine,
        in_specs=(P(ZC, None), P(ZC, XY), P(ZC, XY), P(ZC), P(XY)),
        out_specs=(P(ZC, XY), P(ZC, XY), P(ZC), P(XY)),
        check_vma=False,
    )
```

```python
import jax
import jax.numpy as jnp
from jax import lax
from jax.experimental import pallas as pl
from jax.experimental.pallas import tpu as pltpu
from jax.sharding import Mesh, PartitionSpec as P

D = 8192
F = 16384

decay_rate = 1.0 - 10.0 ** (-0.8)
step_size = 0.05
tiny_eps = 1e-30

NX, NY, NZ = 4, 4, 16
XY, ZC = ("x", "y"), ("z", "c")


def pairs(n, flip):
    return [(i, i ^ flip) for i in range(n)]


def in_order(y, own, one, two, three):
    odd, upper = (y & 1) == 1, (y & 2) == 2
    near = [jnp.where(odd, one, own), jnp.where(odd, own, one)]
    far = [jnp.where(odd, three, two), jnp.where(odd, two, three)]
    first = [jnp.where(upper, q, p) for p, q in zip(near, far)]
    second = [jnp.where(upper, p, q) for p, q in zip(near, far)]
    return jnp.concatenate(first + second, axis=2)


def features_of_rows(inputs, early):
    x, y, c = lax.axis_index("x"), lax.axis_index("y"), lax.axis_index("c")
    tokens = inputs.shape[0] // NY
    part = lax.dynamic_slice_in_dim(inputs, y * tokens, tokens, 0)
    part = part.reshape(tokens, NZ, NX, 128)
    part = lax.dynamic_index_in_dim(part, x, 2, keepdims=False)
    part = lax.all_to_all(part.transpose(1, 0, 2), "z", 0, 0)
    part, early = lax.optimization_barrier((part, early))
    part = lax.all_gather(part, "x", axis=0)
    low, high = part[:2], part[2:]
    own = jnp.where(c == 0, low, high)
    other = lax.ppermute(jnp.where(c == 0, high, low), "c", pairs(2, 1))
    first, second = jnp.where(c == 0, own, other), jnp.where(c == 0, other, own)

    def swap(block, flip):
        return lax.ppermute(block, "y", pairs(NY, flip))

    first_one, second_three = swap(first, 1), swap(second, 3)
    first_three, second_one = swap(first, 3), swap(second, 1)
    first_two, second_two = swap(first_one, 3), swap(second_three, 1)
    return (
        in_order(y, first, first_one, first_two, first_three),
        in_order(y, second, second_one, second_two, second_three),
        early,
    )


CHUNKS = ((0, 2), (2, 4), (6, 4), (10, 4), (14, 2))


def gradient_kernel(
    core_ref, first_hbm, second_hbm, cot_hbm, grad_hbm, rows_ref, other_hbm,
    first, second, cot, grad, in_sems, out_sems,
):
    fetches = []
    for i, (start, count) in enumerate(CHUNKS):
        planes = pl.ds(start, count)
        fetches.append(
            [
                pltpu.make_async_copy(first_hbm.at[:, planes], first.at[:, planes], in_sems.at[0, i]),
                pltpu.make_async_copy(second_hbm.at[:, planes], second.at[:, planes], in_sems.at[1, i]),
                pltpu.make_async_copy(cot_hbm.at[planes], cot.at[planes], in_sems.at[2, i]),
            ]
        )
        for fetch in fetches[i]:
            fetch.start()
    for i, (start, count) in enumerate(CHUNKS):
        for fetch in fetches[i]:
            fetch.wait()
        feat = [
            jnp.concatenate([ref[0, plane], ref[1, plane]], axis=1)
            for plane in range(start, start + count)
            for ref in (first, second)
        ]
        part = lax.dot_general(
            jnp.concatenate(feat, axis=0),
            cot[start : start + count].reshape(count * 320, 1024),
            (((0,), (0,)), ((), ())),
            preferred_element_type=jnp.float32,
        )
        if i == 0:
            grad[...] = part
        else:
            grad[...] += part
    columns = pl.ds(pl.multiple_of(512 * (1 - core_ref[0, 0]), 512), 512)
    stores = [
        pltpu.make_async_copy(grad.at[:, columns], other_hbm, out_sems.at[0]),
        pltpu.make_async_copy(grad, grad_hbm, out_sems.at[1]),
    ]
    for store in stores:
        store.start()
    squares = jnp.zeros((256, 128), jnp.float32)
    for j in range(8):
        part = grad[:, j * 128 : (j + 1) * 128]
        squares += part * part + tiny_eps
    row = jnp.sum(squares.T, axis=0, keepdims=True)
    for i in range(2 * NX * NY):
        rows_ref[i] = row
    for store in stores:
        store.wait()


LARGE = pltpu.CompilerParams(vmem_limit_bytes=56 * 2**20)
STREAM = pltpu.CompilerParams(vmem_limit_bytes=52 * 2**20 + 943_104)
SMALL = pltpu.CompilerParams(vmem_limit_bytes=16 * 2**20)


VMEM = pl.BlockSpec(memory_space=pltpu.VMEM)
SMEM = pl.BlockSpec(memory_space=pltpu.SMEM)
HBM = pl.BlockSpec(memory_space=pltpu.HBM)


def gradient_of(core, first, second, all_cotangent):
    return pl.pallas_call(
        gradient_kernel,
        in_specs=[SMEM, HBM, HBM, HBM],
        out_specs=[HBM, VMEM, HBM],
        out_shape=[
            jax.ShapeDtypeStruct((256, 1024), jnp.float32),
            jax.ShapeDtypeStruct((2 * NX * NY, 1, 256), jnp.float32),
            jax.ShapeDtypeStruct((256, 512), jnp.float32),
        ],
        scratch_shapes=[
            pltpu.VMEM(first.shape, first.dtype),
            pltpu.VMEM(second.shape, second.dtype),
            pltpu.VMEM(all_cotangent.shape, all_cotangent.dtype),
            pltpu.VMEM((256, 1024), jnp.float32),
            pltpu.SemaphoreType.DMA((3, len(CHUNKS))),
            pltpu.SemaphoreType.DMA((2,)),
        ],
        cost_estimate=pl.CostEstimate(
            flops=2 * 256 * 1024 * 5120, bytes_accessed=15_000_000, transcendentals=0
        ),
        compiler_params=LARGE,
        name="gradient",
    )(core, first, second, all_cotangent)


def rows_kernel(
    core_ref, got_ref, moment_ref, weight_sq_ref, grad_hbm, swapped_ref, new_rows_ref, factor_ref, out_ref, grad, sems
):
    core = core_ref[0, 0]
    columns = pl.ds(pl.multiple_of(512 * core, 512), 512)
    fetches = [
        pltpu.make_async_copy(grad_hbm.at[rows, columns], grad.at[rows], sems.at[i])
        for i, rows in enumerate((pl.ds(0, 128), pl.ds(128, 128)))
    ]
    for fetch in fetches:
        fetch.start()
    new_rows = []
    for half in range(2):
        total = got_ref[half]
        for i in range(1, NX * NY):
            total += got_ref[2 * i + half]
        new_rows.append(decay_rate * moment_ref[half] + (1.0 - decay_rate) * (total / F))
    own = jnp.where(core == 0, new_rows[0], new_rows[1])
    other = jnp.where(core == 0, new_rows[1], new_rows[0])
    new_rows_ref[...] = own
    down = jnp.broadcast_to(own, (128, 256)).T
    factor_ref[...] = lax.rsqrt(down)
    inverse = 1.0 / down
    inverse_other = 1.0 / jnp.broadcast_to(other, (128, 256)).T
    lanes = lax.broadcasted_iota(jnp.int32, (1, 128), 1)
    rows_sum = jnp.sum(own + other, axis=1, keepdims=True)
    scalars = jnp.where(lanes == 0, rows_sum, jnp.where(lanes == 1, weight_sq_ref[0, 0], 0.0))
    for fetch in fetches:
        fetch.wait()
    squares, weighted = [], []
    for j in range(4):
        here = slice(128 * j, 128 * (j + 1))
        mine, theirs = grad[:, here], swapped_ref[:, here]
        mine, theirs = mine * mine, theirs * theirs
        squares.append(jnp.sum((mine + tiny_eps) + (theirs + tiny_eps), axis=0, keepdims=True))
        weighted.append(jnp.sum(mine * inverse + theirs * inverse_other, axis=0, keepdims=True))
    row = jnp.concatenate(squares + weighted + [scalars], axis=1)
    for i in range(NZ):
        out_ref[i] = row


def rows_call(core, row_sums, row_moment, weight_sq, gradient, swapped):
    return pl.pallas_call(
        rows_kernel,
        in_specs=[SMEM, VMEM, VMEM, SMEM, HBM, VMEM],
        out_specs=[VMEM] * 3,
        out_shape=[
            jax.ShapeDtypeStruct((1, 256), jnp.float32),
            jax.ShapeDtypeStruct((256, 128), jnp.float32),
            jax.ShapeDtypeStruct((NZ, 1, 1152), jnp.float32),
        ],
        scratch_shapes=[pltpu.VMEM((256, 512), jnp.float32), pltpu.SemaphoreType.DMA((2,))],
        compiler_params=STREAM,
        name="rows",
    )(core, row_sums, row_moment, weight_sq, gradient, swapped)


def columns_kernel(got_ref, moment_ref, new_cols_ref, scalars_ref, out_ref):
    total = jnp.sum(got_ref[...], axis=0)
    new_cols = decay_rate * moment_ref[...] + (1.0 - decay_rate) * (total[:, :512] / D)
    new_cols_ref[...] = new_cols
    row_mean = total[:, 1024:1025] / D
    scaled_sq = row_mean * jnp.sum(total[:, 512:1024] / new_cols, axis=1, keepdims=True)
    lanes = lax.broadcasted_iota(jnp.int32, (1, 128), 1)
    scalars_ref[...] = jnp.broadcast_to(row_mean, (1, 128))
    weight_sq = total[:, 1025:1026]
    row = jnp.where(lanes == 0, scaled_sq, jnp.where(lanes == 1, weight_sq, 0.0))
    for i in range(2 * NX * NY):
        out_ref[i] = row


def columns_call(packed, half_moment):
    return pl.pallas_call(
        columns_kernel,
        in_specs=[VMEM] * 2,
        out_specs=[VMEM] * 3,
        out_shape=[
            jax.ShapeDtypeStruct((1, 512), jnp.float32),
            jax.ShapeDtypeStruct((1, 128), jnp.float32),
            jax.ShapeDtypeStruct((2 * NX * NY, 1, 128), jnp.float32),
        ],
        compiler_params=SMALL,
        name="columns",
    )(packed, half_moment)


PARTS = 4


def update_kernel(
    got_ref, mean_ref, factor_ref, cols_ref, grad_hbm, weight_hbm, new_weight_hbm, update_hbm,
    cols_hbm, grad, weight, new_weight, update, in_sems, out_sems, cols_sem,
):
    height = 256 // PARTS
    blocks = [pl.ds(i * height, height) for i in range(PARTS)]
    fetches, stores = [], []
    for i, rows in enumerate(blocks):
        fetches.append(pltpu.make_async_copy(grad_hbm.at[rows], grad.at[rows], in_sems.at[0, i]))
        fetches.append(pltpu.make_async_copy(weight_hbm.at[rows], weight.at[rows], in_sems.at[1, i]))
    for fetch in fetches:
        fetch.start()
    stores.append(pltpu.make_async_copy(cols_ref, cols_hbm, cols_sem))
    stores[0].start()
    total = jnp.sum(got_ref[...], axis=0)
    update_rms = jnp.sqrt(total[:, 0:1] / (D * F))
    weight_rms = jnp.sqrt(total[:, 1:2] / (D * F))
    scale = jnp.sqrt(mean_ref[:, 0:1]) / jnp.maximum(1.0, update_rms)
    step = step_size * weight_rms
    cols = [lax.rsqrt(cols_ref[half]) * scale for half in range(2)]
    for i, rows in enumerate(blocks):
        fetches[2 * i].wait()
        fetches[2 * i + 1].wait()
        factor = factor_ref[rows]
        for j in range(8):
            here = slice(j * 128, (j + 1) * 128)
            half = slice((j % 4) * 128, (j % 4 + 1) * 128)
            clipped = grad[rows, here] * factor * cols[j // 4][:, half]
            update[rows, here] = clipped.astype(jnp.bfloat16)
            new_weight[rows, here] = weight[rows, here] - step * clipped
        out = [
            pltpu.make_async_copy(new_weight.at[rows], new_weight_hbm.at[rows], out_sems.at[0, i]),
            pltpu.make_async_copy(update.at[rows], update_hbm.at[rows], out_sems.at[1, i]),
        ]
        for store in out:
            store.start()
        stores += out
    for store in stores:
        store.wait()


def update_call(last, row_mean, row_factor, new_cols, gradient, weight):
    whole = lambda dtype: pltpu.VMEM((256, 1024), dtype)
    return pl.pallas_call(
        update_kernel,
        in_specs=[VMEM] * 4 + [HBM] * 2,
        out_specs=[HBM] * 3,
        out_shape=[
            jax.ShapeDtypeStruct((256, 1024), jnp.float32),
            jax.ShapeDtypeStruct((256, 1024), jnp.bfloat16),
            jax.ShapeDtypeStruct((2, 1, 512), jnp.float32),
        ],
        scratch_shapes=[
            whole(jnp.float32),
            whole(jnp.float32),
            whole(jnp.float32),
            whole(jnp.bfloat16),
            pltpu.SemaphoreType.DMA((2, PARTS)),
            pltpu.SemaphoreType.DMA((2, PARTS)),
            pltpu.SemaphoreType.DMA,
        ],
        compiler_params=STREAM,
        name="update",
    )(last, row_mean, row_factor, new_cols, gradient, weight)


def on_device(inputs, cotangent, weight, row_moment, col_moment):
    c = lax.axis_index("c")
    core = c.astype(jnp.int32).reshape(1, 1)
    all_cotangent = lax.all_gather(cotangent, ZC, axis=0).reshape(NZ, 2, *cotangent.shape)
    early = (jnp.sum(weight * weight), lax.all_gather(row_moment[None], "c", axis=0))
    first, second, (weight_sq, row_moments) = features_of_rows(inputs, early)
    gradient, row_sums, swapped = gradient_of(core, first, second, all_cotangent)
    row_sums = lax.all_to_all(row_sums, ("x", "y", "c"), 0, 0)
    swapped = lax.ppermute(swapped, "c", pairs(2, 1))
    new_rows, row_factor, packed = rows_call(
        core, row_sums, row_moments, weight_sq.reshape(1, 1), gradient, swapped
    )
    packed = lax.all_to_all(packed, "z", 0, 0)
    half_moment = jnp.where(c == 0, col_moment[:512], col_moment[512:])
    half_cols, row_mean, last = columns_call(packed, half_moment[None])
    last = lax.all_to_all(last, ("x", "y", "c"), 0, 0)
    new_cols = lax.all_gather(half_cols, "c", axis=0)
    new_weight, update, new_cols = update_call(
        last, row_mean, row_factor, new_cols, gradient, weight
    )
    return (new_weight, update, new_rows[0], new_cols.reshape(1024))


def solution(mesh):
    fine = Mesh(mesh.devices.reshape(NX, NY, NZ, 2), ("x", "y", "z", "c"))
    return jax.shard_map(
        on_device,
        mesh=fine,
        in_specs=(P(ZC, None), P(ZC, XY), P(ZC, XY), P(ZC), P(XY)),
        out_specs=(P(ZC, XY), P(ZC, XY), P(ZC), P(XY)),
        check_vma=False,
    )
```

```python
import jax
import jax.numpy as jnp
from jax import lax
from jax.experimental import pallas as pl
from jax.experimental.pallas import tpu as pltpu
from jax.sharding import Mesh, PartitionSpec as P

D = 8192
F = 16384

decay_rate = 1.0 - 10.0 ** (-0.8)
step_size = 0.05
tiny_eps = 1e-30

NX, NY, NZ = 4, 4, 16
XY, ZC = ("x", "y"), ("z", "c")


def pairs(n, flip):
    return [(i, i ^ flip) for i in range(n)]


def in_order(y, own, one, two, three):
    odd, upper = (y & 1) == 1, (y & 2) == 2
    near = [jnp.where(odd, one, own), jnp.where(odd, own, one)]
    far = [jnp.where(odd, three, two), jnp.where(odd, two, three)]
    first = [jnp.where(upper, q, p) for p, q in zip(near, far)]
    second = [jnp.where(upper, p, q) for p, q in zip(near, far)]
    return jnp.concatenate(first + second, axis=2)


def features_of_rows(inputs, early):
    x, y, c = lax.axis_index("x"), lax.axis_index("y"), lax.axis_index("c")
    tokens = inputs.shape[0] // NY
    part = lax.dynamic_slice_in_dim(inputs, y * tokens, tokens, 0)
    part = part.reshape(tokens, NZ, NX, 128)
    part = lax.dynamic_index_in_dim(part, x, 2, keepdims=False)
    part = lax.all_to_all(part.transpose(1, 0, 2), "z", 0, 0)
    part, early = lax.optimization_barrier((part, early))
    part = lax.all_gather(part, "x", axis=0)
    low, high = part[:2], part[2:]
    own = jnp.where(c == 0, low, high)
    other = lax.ppermute(jnp.where(c == 0, high, low), "c", pairs(2, 1))
    first, second = jnp.where(c == 0, own, other), jnp.where(c == 0, other, own)

    def swap(block, flip):
        return lax.ppermute(block, "y", pairs(NY, flip))

    first_one, second_three = swap(first, 1), swap(second, 3)
    first_three, second_one = swap(first, 3), swap(second, 1)
    first_two, second_two = swap(first_one, 3), swap(second_three, 1)
    return (
        in_order(y, first, first_one, first_two, first_three),
        in_order(y, second, second_one, second_two, second_three),
        early,
    )


CHUNKS = ((0, 2), (2, 4), (6, 4), (10, 4), (14, 2))


def gradient_kernel(
    core_ref, first_hbm, second_hbm, cot_hbm, grad_hbm, rows_ref, other_hbm, mine_ref,
    first, second, cot, grad, in_sems, out_sems,
):
    fetches = []
    for i, (start, count) in enumerate(CHUNKS):
        planes = pl.ds(start, count)
        fetches.append(
            [
                pltpu.make_async_copy(first_hbm.at[:, planes], first.at[:, planes], in_sems.at[0, i]),
                pltpu.make_async_copy(second_hbm.at[:, planes], second.at[:, planes], in_sems.at[1, i]),
                pltpu.make_async_copy(cot_hbm.at[planes], cot.at[planes], in_sems.at[2, i]),
            ]
        )
        for fetch in fetches[i]:
            fetch.start()
    for i, (start, count) in enumerate(CHUNKS):
        for fetch in fetches[i]:
            fetch.wait()
        feat = [
            jnp.concatenate([ref[0, plane], ref[1, plane]], axis=1)
            for plane in range(start, start + count)
            for ref in (first, second)
        ]
        part = lax.dot_general(
            jnp.concatenate(feat, axis=0),
            cot[start : start + count].reshape(count * 320, 1024),
            (((0,), (0,)), ((), ())),
            preferred_element_type=jnp.float32,
        )
        if i == 0:
            grad[...] = part
        else:
            grad[...] += part
    columns = pl.ds(pl.multiple_of(512 * (1 - core_ref[0, 0]), 512), 512)
    stores = [
        pltpu.make_async_copy(grad.at[:, columns], other_hbm, out_sems.at[0]),
        pltpu.make_async_copy(grad, grad_hbm, out_sems.at[1]),
    ]
    for store in stores:
        store.start()
    mine_ref[...] = grad[:, pl.ds(pl.multiple_of(512 * core_ref[0, 0], 512), 512)]
    squares = jnp.zeros((256, 128), jnp.float32)
    for j in range(8):
        part = grad[:, j * 128 : (j + 1) * 128]
        squares += part * part + tiny_eps
    row = jnp.sum(squares.T, axis=0, keepdims=True)
    for i in range(2 * NX * NY):
        rows_ref[i] = row
    for store in stores:
        store.wait()


LARGE = pltpu.CompilerParams(vmem_limit_bytes=56 * 2**20)
STREAM = pltpu.CompilerParams(vmem_limit_bytes=52 * 2**20 + 943_104)
SMALL = pltpu.CompilerParams(vmem_limit_bytes=16 * 2**20)


VMEM = pl.BlockSpec(memory_space=pltpu.VMEM)
SMEM = pl.BlockSpec(memory_space=pltpu.SMEM)
HBM = pl.BlockSpec(memory_space=pltpu.HBM)


def gradient_of(core, first, second, all_cotangent):
    return pl.pallas_call(
        gradient_kernel,
        in_specs=[SMEM, HBM, HBM, HBM],
        out_specs=[HBM, VMEM, HBM, VMEM],
        out_shape=[
            jax.ShapeDtypeStruct((256, 1024), jnp.float32),
            jax.ShapeDtypeStruct((2 * NX * NY, 1, 256), jnp.float32),
            jax.ShapeDtypeStruct((256, 512), jnp.float32),
            jax.ShapeDtypeStruct((256, 512), jnp.float32),
        ],
        scratch_shapes=[
            pltpu.VMEM(first.shape, first.dtype),
            pltpu.VMEM(second.shape, second.dtype),
            pltpu.VMEM(all_cotangent.shape, all_cotangent.dtype),
            pltpu.VMEM((256, 1024), jnp.float32),
            pltpu.SemaphoreType.DMA((3, len(CHUNKS))),
            pltpu.SemaphoreType.DMA((2,)),
        ],
        cost_estimate=pl.CostEstimate(
            flops=2 * 256 * 1024 * 5120, bytes_accessed=15_000_000, transcendentals=0
        ),
        compiler_params=STREAM,
        name="gradient",
    )(core, first, second, all_cotangent)


def rows_kernel(
    core_ref, got_ref, moment_ref, weight_sq_ref, mine_ref, swapped_ref, new_rows_ref, factor_ref, out_ref
):
    core = core_ref[0, 0]
    new_rows = []
    for half in range(2):
        total = got_ref[half]
        for i in range(1, NX * NY):
            total += got_ref[2 * i + half]
        new_rows.append(decay_rate * moment_ref[half] + (1.0 - decay_rate) * (total / F))
    own = jnp.where(core == 0, new_rows[0], new_rows[1])
    other = jnp.where(core == 0, new_rows[1], new_rows[0])
    new_rows_ref[...] = own
    down = jnp.broadcast_to(own, (128, 256)).T
    factor_ref[...] = lax.rsqrt(down)
    inverse = 1.0 / down
    inverse_other = 1.0 / jnp.broadcast_to(other, (128, 256)).T
    lanes = lax.broadcasted_iota(jnp.int32, (1, 128), 1)
    rows_sum = jnp.sum(own + other, axis=1, keepdims=True)
    scalars = jnp.where(lanes == 0, rows_sum, jnp.where(lanes == 1, weight_sq_ref[0, 0], 0.0))
    squares, weighted = [], []
    for j in range(4):
        here = slice(128 * j, 128 * (j + 1))
        mine, theirs = mine_ref[:, here], swapped_ref[:, here]
        mine, theirs = mine * mine, theirs * theirs
        squares.append(jnp.sum((mine + tiny_eps) + (theirs + tiny_eps), axis=0, keepdims=True))
        weighted.append(jnp.sum(mine * inverse + theirs * inverse_other, axis=0, keepdims=True))
    row = jnp.concatenate(squares + weighted + [scalars], axis=1)
    for i in range(NZ):
        out_ref[i] = row


def rows_call(core, row_sums, row_moment, weight_sq, mine, swapped):
    return pl.pallas_call(
        rows_kernel,
        in_specs=[SMEM, VMEM, VMEM, SMEM, VMEM, VMEM],
        out_specs=[VMEM] * 3,
        out_shape=[
            jax.ShapeDtypeStruct((1, 256), jnp.float32),
            jax.ShapeDtypeStruct((256, 128), jnp.float32),
            jax.ShapeDtypeStruct((NZ, 1, 1152), jnp.float32),
        ],
        compiler_params=STREAM,
        name="rows",
    )(core, row_sums, row_moment, weight_sq, mine, swapped)


def columns_kernel(got_ref, moment_ref, new_cols_ref, scalars_ref, out_ref):
    total = jnp.sum(got_ref[...], axis=0)
    new_cols = decay_rate * moment_ref[...] + (1.0 - decay_rate) * (total[:, :512] / D)
    new_cols_ref[...] = new_cols
    row_mean = total[:, 1024:1025] / D
    scaled_sq = row_mean * jnp.sum(total[:, 512:1024] / new_cols, axis=1, keepdims=True)
    lanes = lax.broadcasted_iota(jnp.int32, (1, 128), 1)
    scalars_ref[...] = jnp.broadcast_to(row_mean, (1, 128))
    weight_sq = total[:, 1025:1026]
    row = jnp.where(lanes == 0, scaled_sq, jnp.where(lanes == 1, weight_sq, 0.0))
    for i in range(2 * NX * NY):
        out_ref[i] = row


def columns_call(packed, half_moment):
    return pl.pallas_call(
        columns_kernel,
        in_specs=[VMEM] * 2,
        out_specs=[VMEM] * 3,
        out_shape=[
            jax.ShapeDtypeStruct((1, 512), jnp.float32),
            jax.ShapeDtypeStruct((1, 128), jnp.float32),
            jax.ShapeDtypeStruct((2 * NX * NY, 1, 128), jnp.float32),
        ],
        compiler_params=SMALL,
        name="columns",
    )(packed, half_moment)


PARTS = 4


def update_kernel(
    got_ref, mean_ref, factor_ref, cols_ref, grad_hbm, weight_hbm, new_weight_hbm, update_hbm,
    cols_hbm, grad, weight, new_weight, update, in_sems, out_sems, cols_sem,
):
    height = 256 // PARTS
    blocks = [pl.ds(i * height, height) for i in range(PARTS)]
    fetches, stores = [], []
    for i, rows in enumerate(blocks):
        fetches.append(pltpu.make_async_copy(grad_hbm.at[rows], grad.at[rows], in_sems.at[0, i]))
        fetches.append(pltpu.make_async_copy(weight_hbm.at[rows], weight.at[rows], in_sems.at[1, i]))
    for fetch in fetches:
        fetch.start()
    stores.append(pltpu.make_async_copy(cols_ref, cols_hbm, cols_sem))
    stores[0].start()
    total = jnp.sum(got_ref[...], axis=0)
    update_rms = jnp.sqrt(total[:, 0:1] / (D * F))
    weight_rms = jnp.sqrt(total[:, 1:2] / (D * F))
    scale = jnp.sqrt(mean_ref[:, 0:1]) / jnp.maximum(1.0, update_rms)
    step = step_size * weight_rms
    cols = [lax.rsqrt(cols_ref[half]) * scale for half in range(2)]
    for i, rows in enumerate(blocks):
        fetches[2 * i].wait()
        fetches[2 * i + 1].wait()
        factor = factor_ref[rows]
        for j in range(8):
            here = slice(j * 128, (j + 1) * 128)
            half = slice((j % 4) * 128, (j % 4 + 1) * 128)
            clipped = grad[rows, here] * factor * cols[j // 4][:, half]
            update[rows, here] = clipped.astype(jnp.bfloat16)
            new_weight[rows, here] = weight[rows, here] - step * clipped
        out = [
            pltpu.make_async_copy(new_weight.at[rows], new_weight_hbm.at[rows], out_sems.at[0, i]),
            pltpu.make_async_copy(update.at[rows], update_hbm.at[rows], out_sems.at[1, i]),
        ]
        for store in out:
            store.start()
        stores += out
    for store in stores:
        store.wait()


def update_call(last, row_mean, row_factor, new_cols, gradient, weight):
    whole = lambda dtype: pltpu.VMEM((256, 1024), dtype)
    return pl.pallas_call(
        update_kernel,
        in_specs=[VMEM] * 4 + [HBM] * 2,
        out_specs=[HBM] * 3,
        out_shape=[
            jax.ShapeDtypeStruct((256, 1024), jnp.float32),
            jax.ShapeDtypeStruct((256, 1024), jnp.bfloat16),
            jax.ShapeDtypeStruct((2, 1, 512), jnp.float32),
        ],
        scratch_shapes=[
            whole(jnp.float32),
            whole(jnp.float32),
            whole(jnp.float32),
            whole(jnp.bfloat16),
            pltpu.SemaphoreType.DMA((2, PARTS)),
            pltpu.SemaphoreType.DMA((2, PARTS)),
            pltpu.SemaphoreType.DMA,
        ],
        compiler_params=STREAM,
        name="update",
    )(last, row_mean, row_factor, new_cols, gradient, weight)


def on_device(inputs, cotangent, weight, row_moment, col_moment):
    c = lax.axis_index("c")
    core = c.astype(jnp.int32).reshape(1, 1)
    all_cotangent = lax.all_gather(cotangent, ZC, axis=0).reshape(NZ, 2, *cotangent.shape)
    early = (jnp.sum(weight * weight), lax.all_gather(row_moment[None], "c", axis=0))
    first, second, (weight_sq, row_moments) = features_of_rows(inputs, early)
    gradient, row_sums, swapped, mine = gradient_of(core, first, second, all_cotangent)
    row_sums = lax.all_to_all(row_sums, ("x", "y", "c"), 0, 0)
    swapped = lax.ppermute(swapped, "c", pairs(2, 1))
    new_rows, row_factor, packed = rows_call(
        core, row_sums, row_moments, weight_sq.reshape(1, 1), mine, swapped
    )
    packed = lax.all_to_all(packed, "z", 0, 0)
    half_moment = jnp.where(c == 0, col_moment[:512], col_moment[512:])
    half_cols, row_mean, last = columns_call(packed, half_moment[None])
    last = lax.all_to_all(last, ("x", "y", "c"), 0, 0)
    new_cols = lax.all_gather(half_cols, "c", axis=0)
    new_weight, update, new_cols = update_call(
        last, row_mean, row_factor, new_cols, gradient, weight
    )
    return (new_weight, update, new_rows[0], new_cols.reshape(1024))


def solution(mesh):
    fine = Mesh(mesh.devices.reshape(NX, NY, NZ, 2), ("x", "y", "z", "c"))
    return jax.shard_map(
        on_device,
        mesh=fine,
        in_specs=(P(ZC, None), P(ZC, XY), P(ZC, XY), P(ZC), P(XY)),
        out_specs=(P(ZC, XY), P(ZC, XY), P(ZC), P(XY)),
        check_vma=False,
    )
```
